256 devices in a mesh: row: 8 (over y, core), blk: 32 (over x, z).
Axes of the slice: x: 4, y: 4, z: 8, core: 2. Of those that a mesh axis runs over, the one named last changes fastest.
Arguments:
- theta: float32 [32, 32, 256, 256], P('blk'), may hold values from -6 to 6
- left_env: float32 [16, 32, 256, 256], P('row', 'blk'), may hold values from -0.375 to 0.375
- right_env: float32 [16, 32, 256, 256], P('row', 'blk'), may hold values from -0.375 to 0.375
- left_tiles: int32 [32], replicated, may hold values from 1 to 4
- right_tiles: int32 [32], replicated, may hold values from 1 to 4
- pairs: int32 [48, 2], replicated, may hold values from 0 to 15
- coefs: float32 [48], replicated, may hold values from -2 to 2
Outputs:
- hpsi: float32 [32, 32, 256, 256], P('blk', None, 'row')
The draws below stay inside these ranges and needn't reach their ends.
All inputs are finite; a program needn't handle non-finite values.
Results may differ from the reference program's by a relative error of at most 0.000071.
Values sent between devices are 32-bit elements; how exact they have to be, the bound alone decides.
A program may use at most 128 MiB of HBM per device.

```python
import jax
import jax.numpy as jnp
from jax import lax

MB = 256
NW = 16
KP = 48
NP = 32
NQ = 32


def with_ends(entries, own_key, low, largest):
    index_at = [jax.random.randint(jax.random.fold_in(own_key, axis), (), 0, length) for axis, length in enumerate(entries.shape)]
    main_axis = entries.shape.index(max(entries.shape))
    beside = index_at[:main_axis] + [(index_at[main_axis] + 1) % entries.shape[main_axis]] + index_at[main_axis + 1:]
    return entries.at[tuple(index_at)].set(low).at[tuple(beside)].set(largest)


def block_levels(stream_key, extent, cuts, low, top_value):
    def one(position, blocks):
        draws = jax.random.uniform(jax.random.fold_in(jax.random.fold_in(stream_key, 6), position), (blocks,), jnp.float32, low / len(cuts), top_value / len(cuts))
        return jnp.repeat(jnp.exp(draws), extent[position] // blocks).reshape((-1,) + (1,) * (len(extent) - position - 1))

    loudness = one(*cuts[0])
    for cut in cuts[1:]:
        loudness = loudness * one(*cut)
    return loudness


def bell_draw(rng, shape, deviation, bound, split=(), kind=jnp.bfloat16):
    loudness = block_levels(rng, shape, split, -0.22, 0.18) if split else 1.0
    drawn = jax.random.normal(rng, shape, jnp.float32) * deviation * loudness
    return jnp.minimum(jnp.maximum(drawn, -bound), bound).astype(kind)


def setup_inputs(seed: int = 0) -> dict:
    streams_of = jax.random.split(jax.random.key(seed), 8)
    return {
        "theta": bell_draw(streams_of[0], (NP, NQ, MB, MB), 1.0, 6.0, ((0, 32),), jnp.float32),
        "left_env": bell_draw(streams_of[1], (NW, NP, MB, MB), MB ** -0.5, 0.375, ((0, 8), (1, 32)), jnp.float32),
        "right_env": bell_draw(streams_of[2], (NW, NQ, MB, MB), MB ** -0.5, 0.375, ((0, 8), (1, 32)), jnp.float32),
        "left_tiles": with_ends(jax.random.randint(streams_of[3], (NP,), 1, 5), jax.random.fold_in(streams_of[3], 1), 1, 4).astype(jnp.int32),
        "right_tiles": with_ends(jax.random.randint(streams_of[4], (NQ,), 1, 5), jax.random.fold_in(streams_of[4], 1), 1, 4).astype(jnp.int32),
        "pairs": with_ends(jax.random.randint(streams_of[5], (KP, 2), 0, NW), jax.random.fold_in(streams_of[5], 1), 0, NW - 1).astype(jnp.int32),
        "coefs": bell_draw(streams_of[6], (KP,), 0.15, 2.0, (), jnp.float32),
    }


def reference(theta, left_env, right_env, left_tiles, right_tiles, pairs, coefs):
    quarter = MB // 4
    cells = jnp.arange(MB).astype(jnp.int32)
    left_mask = (cells[None, :] < quarter * left_tiles[:, None]).astype(jnp.float32)
    right_mask = (cells[None, :] < quarter * right_tiles[:, None]).astype(jnp.float32)
    masked = theta * left_mask[:, None, :, None] * right_mask[None, :, None, :]
    bonds = jnp.arange(NW).astype(jnp.int32)
    onehot_left = (pairs[:, 0][:, None] == bonds[None, :]).astype(jnp.float32)
    onehot_right = (pairs[:, 1][:, None] == bonds[None, :]).astype(jnp.float32)
    couplings = jnp.einsum("ka,kb->ab", onehot_left * coefs[:, None], onehot_right, precision=lax.Precision.HIGHEST)
    dressed = jnp.einsum("ab,bqij->aqij", couplings, right_env, precision=lax.Precision.HIGHEST)

    def per_left(index):
        panel = left_env[:, index]
        blocks = masked[index]
        partial_value = jnp.einsum("aij,qjk->aqik", panel, blocks, precision=lax.Precision.HIGHEST)
        return jnp.einsum("aqik,aqlk->qil", partial_value, dressed, precision=lax.Precision.HIGHEST)

    summed = lax.map(per_left, jnp.arange(NP).astype(jnp.int32))
    return summed * left_mask[:, None, :, None] * right_mask[None, :, None, :]
```

```python
import functools

import jax
import jax.numpy as jnp
from jax import lax
from jax.experimental import pallas as pl
from jax.experimental.pallas import tpu as pltpu
from jax.sharding import PartitionSpec as P

MESH = pl.DeviceIdType.MESH
F32 = jnp.float32
BF16 = jnp.bfloat16
NX, NY, NZ = 4, 4, 8
MB = 256
SLAB = 32
DIST = (0, 1, 7, 2, 6, 3, 5, 4)
POS = tuple(DIST.index(d) for d in range(8))
GROUPS = ((0, 0), (1, 0), (3, 0), (2, 0), (0, 1), (1, 1), (3, 1), (2, 1))
NG = len(GROUPS)


def pick(table, at):
    return sum((at == i).astype(jnp.int32) * v for i, v in enumerate(table) if v)


def split(v):
    hi = v.astype(BF16)
    return hi, (v - hi.astype(F32)).astype(BF16)


def dot(a, b):
    return jnp.dot(a, b, preferred_element_type=F32)


def kernel(
    coup, lt, rt, th_in, l_in, r_in, o_ref,
    th, rin, rbuf, rhi, rlo, lall, xbuf, xhi, xlo, part, sib, f1, f2, fin,
    loc, own_s, l_s, l_r, z_s, z_r, t_s, t_r, ts_s, ts_r, q_s, q_r, x_s, x_r,
    p_s, p_r, f1_s, f1_r, f2_s, f2_r, o_s, o_r, o_l,
):
    row, blk = lax.axis_index("row"), lax.axis_index("blk")
    y, c = row // 2, row % 2
    x, z = blk // NZ, blk % NZ
    other = 1 - c

    def at(dx=0, dy=0, dz=0, flip=False):
        core = other if flip else c
        return (((y + dy) % NY) * 2 + core, ((x + dx) % NX) * NZ + (z + dz) % NZ)

    yp, ym, y2 = at(dy=1), at(dy=3), at(dy=2)
    xp, xm, x2 = at(dx=1), at(dx=3), at(dx=2)
    zp, zm = at(dz=1), at(dz=7)
    sb = at(flip=True)
    rp, rm, r2 = (row + 2) % 8, (row + 6) % 8, (row + 4) % 8
    srow = y * 2 + other
    sp, sm, s2 = (srow + 2) % 8, (srow + 6) % 8, (srow + 4) % 8

    def rc(src, dst, ss, rs, to):
        return pltpu.make_async_remote_copy(
            src_ref=src, dst_ref=dst, send_sem=ss, recv_sem=rs, device_id=to, device_id_type=MESH
        )

    sends = []
    mine = [2 * k + c for k in range(4)]
    theirs = [2 * k + other for k in range(4)]

    def view(of):
        return of[0].at[of[1]]

    def send(src, dst, ss, rs, to):
        rc(view(src), view(dst), view(ss), view(rs), to).start()
        sends.append((src, ss))

    def got(dst, rs):
        rc(dst, dst, rs, rs, sb).wait_recv()

    def sent(src, ss):
        rc(src, src, ss, ss, sb).wait_send()

    pltpu.make_async_copy(r_in.at[:, 0], rin, loc.at[0]).start()
    pltpu.make_async_copy(l_in.at[:, 0], lall.at[row], loc.at[1]).start()
    for i in range(8):
        pltpu.make_async_copy(
            th_in.at[0, x * NZ + (z + DIST[i]) % NZ], th.at[0, i], own_s.at[i]
        ).start()

    barrier = pltpu.get_barrier_semaphore()
    partners = (yp, ym, xp, xm, x2, zp, zm, sb)
    for t in partners:
        pl.semaphore_signal(barrier, inc=1, device_id=t, device_id_type=MESH)
    pl.semaphore_wait(barrier, len(partners))

    for i, t in enumerate((yp, ym, sb)):
        send((l_in, (slice(None), 0)), (lall, (row,)), (l_s, (i,)), (l_r, (i,)), t)

    def theta_at(xx, i):
        return (th_in, (0, xx * NZ + (z + i) % NZ,))

    def send_theta(k):
        d = DIST[2 * k] + c * (DIST[2 * k + 1] - DIST[2 * k])
        send(theta_at((x + 1) % NX, d), (th, (3, mine[k],)), (t_s, (0, k,)), (t_r, (0, k,)), xp)
        send(theta_at((x + 3) % NX, d), (th, (1, mine[k],)), (t_s, (1, k,)), (t_r, (1, k,)), xm)

    send_theta(0)
    send_theta(1)
    send(theta_at((x + 2) % NX, pick(DIST, row)), (th, (2, row,)), (q_s, (8,)), (q_r, (8,)), x2)

    row_ids = lax.broadcasted_iota(jnp.int32, (MB, MB), 0)
    col_ids = lax.broadcasted_iota(jnp.int32, (MB, MB), 1)
    pltpu.make_async_copy(r_in.at[:, 0], rin, loc.at[0]).wait()
    rlim = (MB // 4) * rt[blk]
    for b in range(2):
        v = jnp.where((row_ids < rlim) & (col_ids < rlim), rin[b], 0.0)
        rbuf[0, b] = v.T

    def z_send(k, b, up):
        if up:
            src, dst = (rbuf, (POS[(8 - k) % 8], b)), (rbuf, (POS[(7 - k) % 8], b))
        else:
            src, dst = (rbuf, (POS[k], b)), (rbuf, (POS[k + 1], b))
        s = 0 if up else 1
        send(src, dst, (z_s, (s, k, b,)), (z_r, (s, k, b,)), zp if up else zm)

    def z_got(k, b, up):
        s = 0 if up else 1
        got(rbuf.at[POS[8 - k] if up else POS[k], b], z_r.at[s, k - 1, b])

    def z_forward(k):
        for b in range(2):
            for up in (True, False):
                z_got(k, b, up)
                if k < 3 or b == (0 if up else 1):
                    z_send(k, b, up)

    for b in range(2):
        z_send(0, b, True)
        z_send(0, b, False)

    def split_r(pos):
        for b in range(2):
            hi, lo = split(rbuf[pos, b])
            rhi[pos, b * MB : (b + 1) * MB, :] = hi
            rlo[pos, b * MB : (b + 1) * MB, :] = lo

    split_r(0)

    got(lall.at[rm], l_r.at[0])
    send((lall, (rm, 0,)), (lall, (rm, 0,)), (l_s, (3,)), (l_r, (3,)), yp)
    send((lall, (rm,)), (lall, (rm,)), (l_s, (5,)), (l_r, (5,)), sb)
    got(lall.at[rp], l_r.at[1])
    send((lall, (rp, 1,)), (lall, (rp, 1,)), (l_s, (4,)), (l_r, (4,)), ym)
    send((lall, (rp,)), (lall, (rp,)), (l_s, (6,)), (l_r, (6,)), sb)

    z_forward(1)

    got(th.at[2, row], q_r.at[8])

    def sib_theta(k):
        for s, dx in ((0, 3), (1, 1)):
            got(th.at[dx, mine[k]], t_r.at[s, k])
            send((th, (dx, mine[k],)), (th, (dx, mine[k],)), (ts_s, (s, k,)), (ts_r, (s, k,)), sb)

    def sib_theta_got(k):
        for s, dx in ((0, 3), (1, 1)):
            got(th.at[dx, theirs[k]], ts_r.at[s, k])

    sib_theta(0)
    sib_theta(1)

    got(lall.at[r2, 0], l_r.at[3])
    got(lall.at[r2, 1], l_r.at[4])
    send((lall, (r2,)), (lall, (r2,)), (l_s, (7,)), (l_r, (7,)), sb)
    for i, t in enumerate((yp, ym, sb)):
        send((th, (2, row,)), (th, (2, row,)), (q_s, (i,)), (q_r, (i,)), t)
    got(lall.at[srow], l_r.at[2])
    got(lall.at[sm], l_r.at[5])
    got(lall.at[sp], l_r.at[6])
    got(lall.at[s2], l_r.at[7])
    pltpu.make_async_copy(l_in.at[:, 0], lall.at[row], loc.at[1]).wait()

    llim = (MB // 4) * lt[blk]
    strip = 32

    @pl.loop(0, MB // strip)
    def _(s):
        first = pl.multiple_of(s * strip, strip)
        rows = lax.broadcasted_iota(jnp.int32, (strip, MB), 0) + first
        cols = lax.broadcasted_iota(jnp.int32, (strip, MB), 1)
        keep = (rows < llim) & (cols < llim)

        def add(r, acc):
            for a in range(2):
                v = lall[r, a, pl.ds(first, strip), :]
                acc = [acc[b] + coup[2 * r + a, 2 * row + b] * v for b in range(2)]
            return acc

        acc = lax.fori_loop(0, 8, add, [jnp.zeros((strip, MB), F32) for _ in range(2)], unroll=True)
        for b in range(2):
            v = jnp.where(keep, acc[b], 0.0)
            xbuf[0, b, pl.ds(first, strip), :] = v
            hi, lo = split(v)
            xhi[0, pl.ds(b * MB + first, strip), :] = hi
            xlo[0, pl.ds(b * MB + first, strip), :] = lo

    for b in range(2):
        send((xbuf, (0, b,)), (xbuf, (3, b,)), (x_s, (0, b,)), (x_r, (0, b,)), xp)
        send((xbuf, (0, b,)), (xbuf, (1, b,)), (x_s, (1, b,)), (x_r, (1, b,)), xm)
    send_theta(2)
    send_theta(3)

    def split_x(dx):
        for b in range(2):
            hi, lo = split(xbuf[dx, b])
            xhi[dx, b * MB : (b + 1) * MB, :] = hi
            xlo[dx, b * MB : (b + 1) * MB, :] = lo

    def event0():
        z_forward(2)
        for i in range(8):
            pltpu.make_async_copy(th_in.at[0, x * NZ + (z + DIST[i]) % NZ], th.at[0, i], own_s.at[i]).wait()
        for pos in (1, 2, 3):
            split_r(pos)
        got(th.at[2, rm], q_r.at[0])
        send((th, (2, rm, pl.ds(0, MB // 2),)), (th, (2, rm, pl.ds(0, MB // 2),)), (q_s, (3,)), (q_r, (3,)), yp)
        send((th, (2, rm,)), (th, (2, rm,)), (q_s, (5,)), (q_r, (5,)), sb)
        got(th.at[2, rp], q_r.at[1])
        send((th, (2, rp, pl.ds(MB // 2, MB // 2),)), (th, (2, rp, pl.ds(MB // 2, MB // 2),)), (q_s, (4,)), (q_r, (4,)), ym)
        send((th, (2, rp,)), (th, (2, rp,)), (q_s, (6,)), (q_r, (6,)), sb)

    def event1():
        got(xbuf.at[3, 0], x_r.at[0, 0])
        send((xbuf, (3, 0,)), (xbuf, (2, 0,)), (x_s, (2, 0,)), (x_r, (2, 0,)), xp)
        got(xbuf.at[1, 0], x_r.at[1, 0])
        got(xbuf.at[1, 1], x_r.at[1, 1])
        send((xbuf, (1, 1,)), (xbuf, (2, 1,)), (x_s, (2, 1,)), (x_r, (2, 1,)), xm)
        split_x(1)
        sib_theta_got(0)
        sib_theta_got(1)

    def event2():
        got(xbuf.at[3, 1], x_r.at[0, 1])
        split_x(3)
        z_forward(3)

    def event3():
        got(th.at[2, r2, pl.ds(0, MB // 2)], q_r.at[3])
        got(th.at[2, r2, pl.ds(MB // 2, MB // 2)], q_r.at[4])
        send((th, (2, r2,)), (th, (2, r2,)), (q_s, (7,)), (q_r, (7,)), sb)
        got(th.at[2, srow], q_r.at[2])
        got(th.at[2, sm], q_r.at[5])
        got(th.at[2, sp], q_r.at[6])
        got(th.at[2, s2], q_r.at[7])
        got(xbuf.at[2, 0], x_r.at[2, 0])
        got(xbuf.at[2, 1], x_r.at[2, 1])
        split_x(2)

    def event4():
        sib_theta(2)
        sib_theta(3)
        z_got(4, 0, True)
        z_got(4, 1, False)
        for pos in (4, 5, 6, 7):
            split_r(pos)

    def event5():
        sib_theta_got(2)
        sib_theta_got(3)

    events = (event0, event1, event2, event3, event4, event5)

    def out_copy(g, j):
        dx, half = pick([a for a, _ in GROUPS], g), pick([h for _, h in GROUPS], g)
        d = pick(DIST, half * 4 + j)
        q = x * NZ + (z + d) % NZ
        return dx, q

    yn, yd, yf = (y + 1) % NY, (y + 3) % NY, (y + 2) % NY

    def stage3(g):
        got(f2.at[g, 0], f2_r.at[g, 0])
        got(f2.at[g, 1], f2_r.at[g, 1])
        fin[g] = part[g, c, y] + f2[g, 0] + f2[g, 1]
        for j in range(4):
            dx, q = out_copy(g, j)

            @pl.when(dx == 0)
            def _():
                pltpu.make_async_copy(fin.at[g, j], o_ref.at[0, q], o_l.at[g, j]).start()

            @pl.when(dx != 0)
            def _():
                to = (row, ((x + dx) % NX) * NZ + z)
                rc(fin.at[g, j], o_ref.at[0, q], o_s.at[g, j], o_r.at[g, j], to).start()

    def stage2(g):
        got(f1.at[g, 0], f1_r.at[g, 0])
        part[g, c, yn, 0:2] = part[g, c, yn, 0:2] + f1[g, 0]
        rc(part.at[g, c, yn], f2.at[g, 0], f2_s.at[g, 0], f2_r.at[g, 0], yp).start()
        got(f1.at[g, 1], f1_r.at[g, 1])
        part[g, c, yd, 2:4] = part[g, c, yd, 2:4] + f1[g, 1]
        rc(part.at[g, c, yd], f2.at[g, 1], f2_s.at[g, 1], f2_r.at[g, 1], ym).start()

    def stage1(g):
        got(sib.at[g], p_r.at[g])
        part[g, c, yf] = part[g, c, yf] + sib[g, yf]
        rc(part.at[g, c, yf, 0:2], f1.at[g, 0], f1_s.at[g, 0], f1_r.at[g, 0], yp).start()
        rc(part.at[g, c, yf, 2:4], f1.at[g, 1], f1_s.at[g, 1], f1_r.at[g, 1], ym).start()
        for yy in (yn, yd, y):
            part[g, c, yy] = part[g, c, yy] + sib[g, yy]

    def compute(g):
        dx, half = pick([a for a, _ in GROUPS], g), pick([h for _, h in GROUPS], g)

        @pl.loop(0, 4)
        def _(j):
            pos = half * 4 + j
            thi, tlo = split(th[dx, pos])
            p = dot(xhi[dx], thi) + dot(xhi[dx], tlo) + dot(xlo[dx], thi)
            wide = jnp.concatenate([p[:MB], p[MB:]], axis=1)
            phi, plo = split(wide)
            o = dot(phi, rhi[pos]) + dot(phi, rlo[pos]) + dot(plo, rhi[pos])
            for s in range(8):
                part[g, s % 2, s // 2, j] = o[s * SLAB : (s + 1) * SLAB, :]

        rc(part.at[g, other], sib.at[g], p_s.at[g], p_r.at[g], sb).start()

    @pl.loop(0, NG + 3)
    def _(g):
        @pl.when(g >= 3)
        def _():
            stage3(g - 3)

        @pl.when((g >= 2) & (g < NG + 2))
        def _():
            stage2(g - 2)

        @pl.when((g >= 1) & (g < NG + 1))
        def _():
            stage1(g - 1)

        for i, event in enumerate(events):
            pl.when(g == i)(event)

        @pl.when(g < NG)
        def _():
            compute(g)

    @pl.loop(0, NG)
    def _(g):
        sent(part.at[g, other], p_s.at[g])
        sent(part.at[g, c, yf, 0:2], f1_s.at[g, 0])
        sent(part.at[g, c, yf, 2:4], f1_s.at[g, 1])
        sent(part.at[g, c, yn], f2_s.at[g, 0])
        sent(part.at[g, c, yd], f2_s.at[g, 1])
        for j in range(4):
            dx, q = out_copy(g, j)
            back = ((x + NX - dx) % NX) * NZ + q % NZ

            @pl.when(dx == 0)
            def _():
                pltpu.make_async_copy(fin.at[g, j], o_ref.at[0, q], o_l.at[g, j]).wait()

            @pl.when(dx != 0)
            def _():
                sent(fin.at[g, j], o_s.at[g, j])
                got(o_ref.at[0, back], o_r.at[g, j])

    for src, ss in sends:
        sent(view(src), view(ss))


def apply(coup, lt, rt, theta, left_env, right_env):
    dma = pltpu.SemaphoreType.DMA
    return pl.pallas_call(
        kernel,
        out_shape=jax.ShapeDtypeStruct((1, NX * NZ, SLAB, MB), F32),
        in_specs=[pl.BlockSpec(memory_space=pltpu.SMEM)] * 3 + [pl.BlockSpec(memory_space=pl.ANY)] * 3,
        out_specs=pl.BlockSpec(memory_space=pl.ANY),
        scratch_shapes=[
            pltpu.VMEM((4, 8, MB, MB), F32),
            pltpu.VMEM((2, MB, MB), F32),
            pltpu.VMEM((8, 2, MB, MB), F32),
            pltpu.VMEM((8, 2 * MB, MB), BF16),
            pltpu.VMEM((8, 2 * MB, MB), BF16),
            pltpu.VMEM((8, 2, MB, MB), F32),
            pltpu.VMEM((4, 2, MB, MB), F32),
            pltpu.VMEM((4, 2 * MB, MB), BF16),
            pltpu.VMEM((4, 2 * MB, MB), BF16),
            pltpu.VMEM((NG, 2, 4, 4, SLAB, MB), F32),
            pltpu.VMEM((NG, 4, 4, SLAB, MB), F32),
            pltpu.VMEM((NG, 2, 2, SLAB, MB), F32),
            pltpu.VMEM((NG, 2, 4, SLAB, MB), F32),
            pltpu.VMEM((NG, 4, SLAB, MB), F32),
            dma((2,)), dma((8,)),
            dma((8,)), dma((8,)),
            dma((2, 4, 2)), dma((2, 4, 2)),
            dma((2, 4)), dma((2, 4)),
            dma((2, 4)), dma((2, 4)),
            dma((9,)), dma((9,)),
            dma((3, 2)), dma((3, 2)),
            dma((NG,)), dma((NG,)),
            dma((NG, 2)), dma((NG, 2)),
            dma((NG, 2)), dma((NG, 2)),
            dma((NG, 4)), dma((NG, 4)), dma((NG, 4)),
        ],
        compiler_params=pltpu.CompilerParams(
            collective_id=0, has_side_effects=True, vmem_limit_bytes=56 * 2**20
        ),
        name="hpsi",
    )(coup, lt, rt, theta, left_env, right_env)


def per_device(theta, left_env, right_env, left_tiles, right_tiles, pairs, coefs):
    bonds = jnp.arange(16)
    onehot_left = (pairs[:, 0][:, None] == bonds[None, :]).astype(F32)
    onehot_right = (pairs[:, 1][:, None] == bonds[None, :]).astype(F32)
    couplings = jnp.einsum(
        "ka,kb->ab", onehot_left * coefs[:, None], onehot_right, precision=lax.Precision.HIGHEST
    )
    return apply(couplings, left_tiles, right_tiles, theta, left_env, right_env)


def solution(mesh):
    return jax.shard_map(
        per_device,
        mesh=mesh,
        in_specs=(
            P("blk", None, None, None),
            P("row", "blk", None, None),
            P("row", "blk", None, None),
            P(),
            P(),
            P(),
            P(),
        ),
        out_specs=P("blk", None, "row", None),
        check_vma=False,
    )
```

```python
import functools

import jax
import jax.numpy as jnp
from jax import lax
from jax.experimental import pallas as pl
from jax.experimental.pallas import tpu as pltpu
from jax.sharding import PartitionSpec as P

MESH = pl.DeviceIdType.MESH
F32 = jnp.float32
BF16 = jnp.bfloat16
NX, NY, NZ = 4, 4, 8
MB = 256
SLAB = 32
DIST = (0, 1, 7, 2, 6, 3, 5, 4)
POS = tuple(DIST.index(d) for d in range(8))
GROUPS = (
    (0, 0), (0, 1), (1, 0), (3, 0), (1, 1), (3, 1), (2, 0), (2, 1),
    (2, 2), (1, 2), (3, 2), (2, 3), (1, 3), (3, 3), (0, 2), (0, 3),
)
TASKS = 2
NG = len(GROUPS)
PARTS = 4
PIECE = MB // PARTS


def pick(table, at):
    return sum((at == i).astype(jnp.int32) * v for i, v in enumerate(table) if v)


def split(v):
    hi = v.astype(BF16)
    return hi, (v - hi.astype(F32)).astype(BF16)


def dot(a, b):
    return jnp.dot(a, b, preferred_element_type=F32)


def kernel(
    pairs, coefs, lt, rt, th_in, l_in, r_in, o_ref,
    th, rin, rbuf, r3, lall, xbuf, x3, part, sib, f1, f2, fin,
    loc, own_s, l_s, l_r, z_s, z_r, t_s, t_r, ts_s, ts_r, q_s, q_r, x_s, x_r,
    p_s, p_r, f1_s, f1_r, f2_s, f2_r, o_s, o_r, o_l,
):
    row, blk = lax.axis_index("row"), lax.axis_index("blk")
    y, c = row // 2, row % 2
    x, z = blk // NZ, blk % NZ
    other = 1 - c

    def at(dx=0, dy=0, dz=0, flip=False):
        core = other if flip else c
        return (((y + dy) % NY) * 2 + core, ((x + dx) % NX) * NZ + (z + dz) % NZ)

    yp, ym, y2 = at(dy=1), at(dy=3), at(dy=2)
    xp, xm, x2 = at(dx=1), at(dx=3), at(dx=2)
    zp, zm = at(dz=1), at(dz=7)
    sb = at(flip=True)
    rp, rm, r2 = (row + 2) % 8, (row + 6) % 8, (row + 4) % 8
    srow = y * 2 + other
    sp, sm, s2 = (srow + 2) % 8, (srow + 6) % 8, (srow + 4) % 8

    def rc(src, dst, ss, rs, to):
        return pltpu.make_async_remote_copy(
            src_ref=src, dst_ref=dst, send_sem=ss, recv_sem=rs, device_id=to, device_id_type=MESH
        )

    sends = []
    mine = [2 * k + c for k in range(4)]
    theirs = [2 * k + other for k in range(4)]

    def view(of):
        return of[0].at[of[1]]

    def send(src, dst, ss, rs, to):
        rc(view(src), view(dst), view(ss), view(rs), to).start()
        sends.append((dst, ss))

    def got(dst, rs):
        rc(dst, dst, rs, rs, sb).wait_recv()

    def sent(src, ss):
        rc(src, src, ss, ss, sb).wait_send()

    H = MB // 2

    def piece(h):
        return l_in, (slice(None), 0, pl.ds(h * PIECE, PIECE))

    pltpu.make_async_copy(r_in.at[:, 0], rin, loc.at[0]).start()
    for h in range(PARTS):
        pltpu.make_async_copy(view(piece(h)), lall.at[h, row], loc.at[1 + h]).start()

    def own_theta(i):
        return pltpu.make_async_copy(
            th_in.at[0, x * NZ + (z + DIST[i]) % NZ], th.at[0, i], own_s.at[i]
        )

    barrier = pltpu.get_barrier_semaphore()
    partners = (yp, ym, xp, xm, x2, zp, zm, sb)
    for t in partners:
        pl.semaphore_signal(barrier, inc=1, device_id=t, device_id_type=MESH)
    pl.semaphore_wait(barrier, len(partners))

    def l_send(src, dst, h, i, to):
        send(src, (lall, dst), (l_s, (h, i)), (l_r, (h, i)), to)

    def l_own(h):
        for i, t in enumerate((yp, ym, sb)):
            l_send(piece(h), (h, row), h, i, t)

    def l_forward(h):
        for i, (r, t) in enumerate(((rm, yp), (rp, ym))):
            got(lall.at[h, r], l_r.at[h, i])
            l_send((lall, (h, r, i)), (h, r, i), h, 3 + i, t)
            l_send((lall, (h, r)), (h, r), h, 5 + i, sb)

    def l_rest(h):
        for i in range(2):
            got(lall.at[h, r2, i], l_r.at[h, 3 + i])
        l_send((lall, (h, r2)), (h, r2), h, 7, sb)
        got(lall.at[h, srow], l_r.at[h, 2])
        got(lall.at[h, sm], l_r.at[h, 5])
        got(lall.at[h, sp], l_r.at[h, 6])
        got(lall.at[h, s2], l_r.at[h, 7])
        pltpu.make_async_copy(view(piece(h)), lall.at[h, row], loc.at[1 + h]).wait()

    def theta_at(xx, i):
        return th_in, (0, xx * NZ + (z + i) % NZ)

    def send_theta(k):
        d = DIST[2 * k] + c * (DIST[2 * k + 1] - DIST[2 * k])
        send(theta_at((x + 1) % NX, d), (th, (3, mine[k])), (t_s, (0, k)), (t_r, (0, k)), xp)
        send(theta_at((x + 3) % NX, d), (th, (1, mine[k])), (t_s, (1, k)), (t_r, (1, k)), xm)

    def sib_theta(k):
        for s, dx in ((0, 3), (1, 1)):
            got(th.at[dx, mine[k]], t_r.at[s, k])
            send((th, (dx, mine[k])), (th, (dx, mine[k])), (ts_s, (s, k)), (ts_r, (s, k)), sb)

    def sib_theta_got(k):
        for s, dx in ((0, 3), (1, 1)):
            got(th.at[dx, theirs[k]], ts_r.at[s, k])

    def z_send(k, b, up):
        if up:
            src, dst = (rbuf, (POS[(8 - k) % 8], b)), (rbuf, (POS[(7 - k) % 8], b))
        else:
            src, dst = (rbuf, (POS[k], b)), (rbuf, (POS[k + 1], b))
        s = 0 if up else 1
        send(src, dst, (z_s, (s, k, b)), (z_r, (s, k, b)), zp if up else zm)

    def z_got(k, b, up):
        s = 0 if up else 1
        got(rbuf.at[POS[8 - k] if up else POS[k], b], z_r.at[s, k - 1, b])

    def zf(k, b):
        for up in (True, False):
            z_got(k, b, up)
            if k < 3 or b == (0 if up else 1):
                z_send(k, b, up)

    def z_forward(k):
        zf(k, 0)
        zf(k, 1)

    def split_r(pos):
        for b in range(2):
            hi, lo = split(rbuf[pos, b])
            r3[pos, b * MB : (b + 1) * MB, :] = hi
            r3[pos, (2 + b) * MB : (3 + b) * MB, :] = lo
            r3[pos, (4 + b) * MB : (5 + b) * MB, :] = hi

    def store_x(dx, b, first, rows, v):
        hi, lo = split(v)
        at = pl.ds(b * MB + first, rows)
        x3[dx, at, 0:MB] = hi
        x3[dx, at, MB : 2 * MB] = hi
        x3[dx, at, 2 * MB : 3 * MB] = lo

    def split_x(dx):
        for h in range(PARTS):
            for b in range(2):
                store_x(dx, b, h * PIECE, PIECE, xbuf[dx, h, b])

    def x_send(h):
        send((xbuf, (0, h)), (xbuf, (3, h)), (x_s, (0, h)), (x_r, (0, h)), xp)
        send((xbuf, (0, h)), (xbuf, (1, h)), (x_s, (1, h)), (x_r, (1, h)), xm)

    def x_forward(h):
        got(xbuf.at[3, h], x_r.at[0, h])
        send((xbuf, (3, h, 0)), (xbuf, (2, h, 0)), (x_s, (2, h)), (x_r, (2, h)), xp)
        got(xbuf.at[1, h], x_r.at[1, h])
        send((xbuf, (1, h, 1)), (xbuf, (2, h, 1)), (x_s, (3, h)), (x_r, (3, h)), xm)

    def x_rest(h):
        got(xbuf.at[2, h, 0], x_r.at[2, h])
        got(xbuf.at[2, h, 1], x_r.at[3, h])

    def q_first():
        d = pick(DIST, row)
        send(theta_at((x + 2) % NX, d), (th, (2, row)), (q_s, (8,)), (q_r, (8,)), x2)

    def q_own():
        got(th.at[2, row], q_r.at[8])
        for i, t in enumerate((yp, ym, sb)):
            send((th, (2, row)), (th, (2, row)), (q_s, (i,)), (q_r, (i,)), t)

    def q_forward():
        for i, (r, t) in enumerate(((rm, yp), (rp, ym))):
            got(th.at[2, r], q_r.at[i])
            rows = pl.ds(i * H, H)
            send((th, (2, r, rows)), (th, (2, r, rows)), (q_s, (3 + i,)), (q_r, (3 + i,)), t)
            send((th, (2, r)), (th, (2, r)), (q_s, (5 + i,)), (q_r, (5 + i,)), sb)

    def q_rest():
        for i in range(2):
            got(th.at[2, r2, pl.ds(i * H, H)], q_r.at[3 + i])
        send((th, (2, r2)), (th, (2, r2)), (q_s, (7,)), (q_r, (7,)), sb)
        got(th.at[2, srow], q_r.at[2])
        got(th.at[2, sm], q_r.at[5])
        got(th.at[2, sp], q_r.at[6])
        got(th.at[2, s2], q_r.at[7])

    row_ids = lax.broadcasted_iota(jnp.int32, (MB, MB), 0)
    col_ids = lax.broadcasted_iota(jnp.int32, (MB, MB), 1)
    rlim = (MB // 4) * rt[blk]

    def own_r():
        pltpu.make_async_copy(r_in.at[:, 0], rin, loc.at[0]).wait()
        for b in range(2):
            v = jnp.where((row_ids < rlim) & (col_ids < rlim), rin[b], 0.0)
            rbuf[0, b] = v.T
            z_send(0, b, True)
            z_send(0, b, False)
        for i in range(8):
            own_theta(i).start()

    bond = lax.broadcasted_iota(jnp.int32, (16, MB), 0)

    def couple(k, acc):
        here = bond == pairs[k, 0]
        return [
            acc[b] + jnp.where(here & (pairs[k, 1] == 2 * row + b), coefs[k], 0.0) for b in range(2)
        ]

    llim = (MB // 4) * lt[blk]
    strip = 32

    def dress(h):
        @pl.loop(0, PIECE // strip)
        def _(s):
            first = pl.multiple_of(s * strip, strip)
            rows = lax.broadcasted_iota(jnp.int32, (strip, MB), 0) + first + h * PIECE
            cols = lax.broadcasted_iota(jnp.int32, (strip, MB), 1)
            keep = (rows < llim) & (cols < llim)
            acc = [jnp.zeros((strip, MB), F32) for _ in range(2)]
            for a in range(16):
                v = lall[h, a // 2, a % 2, pl.ds(first, strip), :]
                for b in range(2):
                    acc[b] = acc[b] + coup[b][a : a + 1] * v
            for b in range(2):
                v = jnp.where(keep, acc[b], 0.0)
                xbuf[0, h, b, pl.ds(first, strip), :] = v
                store_x(0, b, first + h * PIECE, strip, v)

    def dress_send(h):
        l_rest(h)
        dress(h)
        x_send(h)

    l_own(0)
    l_own(1)
    q_first()
    send_theta(0)
    own_r()
    coup = lax.fori_loop(0, pairs.shape[0], couple, [jnp.zeros((16, MB), F32)] * 2)
    split_r(0)
    l_forward(0)
    l_own(2)
    l_forward(1)
    l_own(3)
    send_theta(1)
    l_forward(2)
    zf(1,0)
    dress_send(0)
    zf(1,1)
    dress_send(1)
    l_forward(3)
    dress_send(2)
    sib_theta(0)
    q_own()
    x_forward(0)
    dress_send(3)
    x_forward(1)
    split_r(1)
    send_theta(2)
    for i in range(8):
        own_theta(i).wait()

    def event1():
        split_r(2)
        x_forward(2)
        zf(2,0)
        zf(2,1)
        split_r(3)

    def event2():
        x_forward(3)
        split_x(1)
        sib_theta_got(0)

    def event3():
        split_x(3)
        q_forward()
        sib_theta(1)
        send_theta(3)

    def event4():
        sib_theta_got(1)

    def event5():
        zf(3,0)
        zf(3,1)

    def event6():
        for h in range(PARTS):
            x_rest(h)
        split_x(2)
        q_rest()

    def event7():
        sib_theta(2)

    def event8():
        split_r(4)
        split_r(5)

    def event9():
        sib_theta_got(2)

    def event10():
        sib_theta(3)

    def event11():
        z_got(4,0,True)
        z_got(4,1,False)
        split_r(6)
        split_r(7)

    def event12():
        sib_theta_got(3)

    events = {1: event1, 2: event2, 3: event3, 4: event4, 5: event5, 6: event6, 7: event7, 8: event8, 9: event9, 10: event10, 11: event11, 12: event12}

    def out_copy(g, j):
        dx, pair = pick([a for a, _ in GROUPS], g), pick([h for _, h in GROUPS], g)
        d = pick(DIST, pair * TASKS + j)
        q = x * NZ + (z + d) % NZ
        return dx, q

    yn, yd, yf = (y + 1) % NY, (y + 3) % NY, (y + 2) % NY

    def stage3(g):
        got(f2.at[g, 0], f2_r.at[g, 0])
        got(f2.at[g, 1], f2_r.at[g, 1])
        fin[g] = part[g, c, y] + f2[g, 0] + f2[g, 1]
        for j in range(TASKS):
            dx, q = out_copy(g, j)

            @pl.when(dx == 0)
            def _():
                pltpu.make_async_copy(fin.at[g, j], o_ref.at[0, q], o_l.at[g, j]).start()

            @pl.when(dx != 0)
            def _():
                to = (row, ((x + dx) % NX) * NZ + z)
                rc(fin.at[g, j], o_ref.at[0, q], o_s.at[g, j], o_r.at[g, j], to).start()

    def stage2(g):
        got(f1.at[g, 0], f1_r.at[g, 0])
        part[g, c, yn, 0] = part[g, c, yn, 0] + f1[g, 0]
        rc(part.at[g, c, yn], f2.at[g, 0], f2_s.at[g, 0], f2_r.at[g, 0], yp).start()
        got(f1.at[g, 1], f1_r.at[g, 1])
        part[g, c, yd, 1] = part[g, c, yd, 1] + f1[g, 1]
        rc(part.at[g, c, yd], f2.at[g, 1], f2_s.at[g, 1], f2_r.at[g, 1], ym).start()

    def stage1(g):
        got(sib.at[g], p_r.at[g])
        part[g, c, yf] = part[g, c, yf] + sib[g, yf]
        rc(part.at[g, c, yf, 0], f1.at[g, 0], f1_s.at[g, 0], f1_r.at[g, 0], yp).start()
        rc(part.at[g, c, yf, 1], f1.at[g, 1], f1_s.at[g, 1], f1_r.at[g, 1], ym).start()
        for yy in (yn, yd, y):
            part[g, c, yy] = part[g, c, yy] + sib[g, yy]

    def compute(g):
        dx, pair = pick([a for a, _ in GROUPS], g), pick([h for _, h in GROUPS], g)

        wides = []
        for j in range(TASKS):
            thi, tlo = split(th[dx, pair * TASKS + j])
            p = dot(x3[dx], jnp.concatenate([thi, tlo, thi], axis=0))
            phi, plo = split(jnp.concatenate([p[:MB], p[MB:]], axis=1))
            wides.append(jnp.concatenate([phi, phi, plo], axis=1))
        for j in range(TASKS):
            o = dot(wides[j], r3[pair * TASKS + j])
            for s in range(8):
                part[g, s % 2, s // 2, j] = o[s * SLAB : (s + 1) * SLAB, :]

        rc(part.at[g, other], sib.at[g], p_s.at[g], p_r.at[g], sb).start()

    @pl.loop(0, NG + 7)
    def _(g):
        @pl.when(g >= 7)
        def _():
            stage3(g - 7)

        @pl.when((g >= 4) & (g < NG + 4))
        def _():
            stage2(g - 4)

        @pl.when((g >= 2) & (g < NG + 2))
        def _():
            stage1(g - 2)

        for i, event in events.items():
            pl.when(g == i)(event)

        @pl.when(g < NG)
        def _():
            compute(g)

    @pl.loop(0, NG)
    def _(g):
        sent(part.at[g, other], p_s.at[g])
        sent(part.at[g, c, yf, 0], f1_s.at[g, 0])
        sent(part.at[g, c, yf, 1], f1_s.at[g, 1])
        sent(part.at[g, c, yn], f2_s.at[g, 0])
        sent(part.at[g, c, yd], f2_s.at[g, 1])
        for j in range(TASKS):
            dx, q = out_copy(g, j)
            back = ((x + NX - dx) % NX) * NZ + q % NZ

            @pl.when(dx == 0)
            def _():
                pltpu.make_async_copy(fin.at[g, j], o_ref.at[0, q], o_l.at[g, j]).wait()

            @pl.when(dx != 0)
            def _():
                sent(fin.at[g, j], o_s.at[g, j])
                got(o_ref.at[0, back], o_r.at[g, j])

    for like, ss in sends:
        sent(view(like), view(ss))


def apply(pairs, coefs, lt, rt, theta, left_env, right_env):
    dma = pltpu.SemaphoreType.DMA
    return pl.pallas_call(
        kernel,
        out_shape=jax.ShapeDtypeStruct((1, NX * NZ, SLAB, MB), F32),
        in_specs=[pl.BlockSpec(memory_space=pltpu.SMEM)] * 4 + [pl.BlockSpec(memory_space=pl.ANY)] * 3,
        out_specs=pl.BlockSpec(memory_space=pl.ANY),
        scratch_shapes=[
            pltpu.VMEM((4, 8, MB, MB), F32),
            pltpu.VMEM((2, MB, MB), F32),
            pltpu.VMEM((8, 2, MB, MB), F32),
            pltpu.VMEM((8, 6 * MB, MB), BF16),
            pltpu.VMEM((PARTS, 8, 2, PIECE, MB), F32),
            pltpu.VMEM((4, PARTS, 2, PIECE, MB), F32),
            pltpu.VMEM((4, 2 * MB, 3 * MB), BF16),
            pltpu.VMEM((NG, 2, 4, TASKS, SLAB, MB), F32),
            pltpu.VMEM((NG, 4, TASKS, SLAB, MB), F32),
            pltpu.VMEM((NG, 2, SLAB, MB), F32),
            pltpu.VMEM((NG, 2, TASKS, SLAB, MB), F32),
            pltpu.VMEM((NG, TASKS, SLAB, MB), F32),
            dma((1 + PARTS,)), dma((8,)),
            dma((PARTS, 8)), dma((PARTS, 8)),
            dma((2, 4, 2)), dma((2, 4, 2)),
            dma((2, 4)), dma((2, 4)),
            dma((2, 4)), dma((2, 4)),
            dma((9,)), dma((9,)),
            dma((4, PARTS)), dma((4, PARTS)),
            dma((NG,)), dma((NG,)),
            dma((NG, 2)), dma((NG, 2)),
            dma((NG, 2)), dma((NG, 2)),
            dma((NG, TASKS)), dma((NG, TASKS)), dma((NG, TASKS)),
        ],
        compiler_params=pltpu.CompilerParams(
            collective_id=0, has_side_effects=True, vmem_limit_bytes=56 * 2**20
        ),
        name="hpsi",
    )(pairs, coefs, lt, rt, theta, left_env, right_env)


def per_device(theta, left_env, right_env, left_tiles, right_tiles, pairs, coefs):
    return apply(pairs, coefs, left_tiles, right_tiles, theta, left_env, right_env)


def solution(mesh):
    return jax.shard_map(
        per_device,
        mesh=mesh,
        in_specs=(
            P("blk", None, None, None),
            P("row", "blk", None, None),
            P("row", "blk", None, None),
            P(),
            P(),
            P(),
            P(),
        ),
        out_specs=P("blk", None, "row", None),
        check_vma=False,
    )
```

```python
import functools

import jax
import jax.numpy as jnp
from jax import lax
from jax.experimental import pallas as pl
from jax.experimental.pallas import tpu as pltpu
from jax.sharding import PartitionSpec as P

MESH = pl.DeviceIdType.MESH
F32 = jnp.float32
BF16 = jnp.bfloat16
NX, NY, NZ = 4, 4, 8
MB = 256
SLAB = 32
DIST = (0, 1, 7, 2, 6, 3, 5, 4)
POS = tuple(DIST.index(d) for d in range(8))
GROUPS = (
    (0, 0), (0, 1), (1, 0), (3, 0), (1, 1), (3, 1), (2, 0), (2, 1),
    (2, 2), (1, 2), (3, 2), (2, 3), (1, 3), (3, 3), (0, 2), (0, 3),
)
TASKS = 2
NG = len(GROUPS)
PARTS = 4
PIECE = MB // PARTS


def pick(table, at):
    return sum((at == i).astype(jnp.int32) * v for i, v in enumerate(table) if v)


def split(v):
    hi = v.astype(BF16)
    return hi, (v - hi.astype(F32)).astype(BF16)


def dot(a, b):
    return jnp.dot(a, b, preferred_element_type=F32)


def kernel(
    pairs, coefs, lt, rt, th_in, l_in, r_in, o_ref,
    th, rin, rbuf, r3, lall, xbuf, x3, part, sib, f1, f2, fin,
    loc, own_s, l_s, l_r, z_s, z_r, t_s, t_r, ts_s, ts_r, q_s, q_r, x_s, x_r,
    p_s, p_r, f1_s, f1_r, f2_s, f2_r, o_s, o_r, o_l,
):
    row, blk = lax.axis_index("row"), lax.axis_index("blk")
    y, c = row // 2, row % 2
    x, z = blk // NZ, blk % NZ
    other = 1 - c

    def at(dx=0, dy=0, dz=0, flip=False):
        core = other if flip else c
        return (((y + dy) % NY) * 2 + core, ((x + dx) % NX) * NZ + (z + dz) % NZ)

    yp, ym, y2 = at(dy=1), at(dy=3), at(dy=2)
    xp, xm, x2 = at(dx=1), at(dx=3), at(dx=2)
    zp, zm = at(dz=1), at(dz=7)
    sb = at(flip=True)
    rp, rm, r2 = (row + 2) % 8, (row + 6) % 8, (row + 4) % 8
    srow = y * 2 + other
    sp, sm, s2 = (srow + 2) % 8, (srow + 6) % 8, (srow + 4) % 8

    def rc(src, dst, ss, rs, to):
        return pltpu.make_async_remote_copy(
            src_ref=src, dst_ref=dst, send_sem=ss, recv_sem=rs, device_id=to, device_id_type=MESH
        )

    sends = []
    mine = [2 * k + c for k in range(4)]
    theirs = [2 * k + other for k in range(4)]

    def view(of):
        return of[0].at[of[1]]

    def send(src, dst, ss, rs, to):
        rc(view(src), view(dst), view(ss), view(rs), to).start()
        sends.append((dst, ss))

    def got(dst, rs):
        rc(dst, dst, rs, rs, sb).wait_recv()

    def sent(src, ss):
        rc(src, src, ss, ss, sb).wait_send()

    H = MB // 2

    def piece(h):
        return l_in, (slice(None), 0, pl.ds(h * PIECE, PIECE))

    pltpu.make_async_copy(r_in.at[:, 0], rin, loc.at[0]).start()
    for h in range(PARTS):
        pltpu.make_async_copy(view(piece(h)), lall.at[h, row], loc.at[1 + h]).start()

    def own_theta(i):
        return pltpu.make_async_copy(
            th_in.at[0, x * NZ + (z + DIST[i]) % NZ], th.at[0, i], own_s.at[i]
        )

    barrier = pltpu.get_barrier_semaphore()
    partners = (yp, ym, xp, xm, x2, zp, zm, sb)
    for t in partners:
        pl.semaphore_signal(barrier, inc=1, device_id=t, device_id_type=MESH)
    pl.semaphore_wait(barrier, len(partners))

    def l_send(src, dst, h, i, to):
        send(src, (lall, dst), (l_s, (h, i)), (l_r, (h, i)), to)

    def l_own(h):
        for i, t in enumerate((yp, ym, sb)):
            l_send(piece(h), (h, row), h, i, t)

    def l_forward(h):
        for i, (r, t) in enumerate(((rm, yp), (rp, ym))):
            got(lall.at[h, r], l_r.at[h, i])
            l_send((lall, (h, r, i)), (h, r, i), h, 3 + i, t)
            l_send((lall, (h, r)), (h, r), h, 5 + i, sb)

    def l_rest(h):
        for i in range(2):
            got(lall.at[h, r2, i], l_r.at[h, 3 + i])
        l_send((lall, (h, r2)), (h, r2), h, 7, sb)
        got(lall.at[h, srow], l_r.at[h, 2])
        got(lall.at[h, sm], l_r.at[h, 5])
        got(lall.at[h, sp], l_r.at[h, 6])
        got(lall.at[h, s2], l_r.at[h, 7])
        pltpu.make_async_copy(view(piece(h)), lall.at[h, row], loc.at[1 + h]).wait()

    def theta_at(xx, i):
        return th_in, (0, xx * NZ + (z + i) % NZ)

    def send_theta(k):
        d = DIST[2 * k] + c * (DIST[2 * k + 1] - DIST[2 * k])
        send(theta_at((x + 1) % NX, d), (th, (3, mine[k])), (t_s, (0, k)), (t_r, (0, k)), xp)
        send(theta_at((x + 3) % NX, d), (th, (1, mine[k])), (t_s, (1, k)), (t_r, (1, k)), xm)

    def sib_theta(k):
        for s, dx in ((0, 3), (1, 1)):
            got(th.at[dx, mine[k]], t_r.at[s, k])
            send((th, (dx, mine[k])), (th, (dx, mine[k])), (ts_s, (s, k)), (ts_r, (s, k)), sb)

    def sib_theta_got(k):
        for s, dx in ((0, 3), (1, 1)):
            got(th.at[dx, theirs[k]], ts_r.at[s, k])

    def z_send(k, b, up):
        if up:
            src, dst = (rbuf, (POS[(8 - k) % 8], b)), (rbuf, (POS[(7 - k) % 8], b))
        else:
            src, dst = (rbuf, (POS[k], b)), (rbuf, (POS[k + 1], b))
        s = 0 if up else 1
        send(src, dst, (z_s, (s, k, b)), (z_r, (s, k, b)), zp if up else zm)

    def z_got(k, b, up):
        s = 0 if up else 1
        got(rbuf.at[POS[8 - k] if up else POS[k], b], z_r.at[s, k - 1, b])

    def zf(k, b):
        for up in (True, False):
            z_got(k, b, up)
            if k < 3 or b == (0 if up else 1):
                z_send(k, b, up)

    def z_forward(k):
        zf(k, 0)
        zf(k, 1)

    def split_r(pos):
        for b in range(2):
            hi, lo = split(rbuf[pos, b])
            r3[pos, b * MB : (b + 1) * MB, :] = hi
            r3[pos, (2 + b) * MB : (3 + b) * MB, :] = lo
            r3[pos, (4 + b) * MB : (5 + b) * MB, :] = hi

    def store_x(dx, b, first, rows, v):
        hi, lo = split(v)
        at = pl.ds(b * MB + first, rows)
        x3[dx, at, 0:MB] = hi
        x3[dx, at, MB : 2 * MB] = hi
        x3[dx, at, 2 * MB : 3 * MB] = lo

    def split_x(dx):
        for h in range(PARTS):
            for b in range(2):
                store_x(dx, b, h * PIECE, PIECE, xbuf[dx, h, b])

    def x_send(h):
        send((xbuf, (0, h)), (xbuf, (3, h)), (x_s, (0, h)), (x_r, (0, h)), xp)
        send((xbuf, (0, h)), (xbuf, (1, h)), (x_s, (1, h)), (x_r, (1, h)), xm)

    def x_forward(h):
        got(xbuf.at[3, h], x_r.at[0, h])
        send((xbuf, (3, h, 0)), (xbuf, (2, h, 0)), (x_s, (2, h)), (x_r, (2, h)), xp)
        got(xbuf.at[1, h], x_r.at[1, h])
        send((xbuf, (1, h, 1)), (xbuf, (2, h, 1)), (x_s, (3, h)), (x_r, (3, h)), xm)

    def x_rest(h):
        got(xbuf.at[2, h, 0], x_r.at[2, h])
        got(xbuf.at[2, h, 1], x_r.at[3, h])

    def q_first():
        d = pick(DIST, row)
        send(theta_at((x + 2) % NX, d), (th, (2, row)), (q_s, (8,)), (q_r, (8,)), x2)

    def q_own():
        got(th.at[2, row], q_r.at[8])
        for i, t in enumerate((yp, ym, sb)):
            send((th, (2, row)), (th, (2, row)), (q_s, (i,)), (q_r, (i,)), t)

    def q_forward():
        for i, (r, t) in enumerate(((rm, yp), (rp, ym))):
            got(th.at[2, r], q_r.at[i])
            rows = pl.ds(i * H, H)
            send((th, (2, r, rows)), (th, (2, r, rows)), (q_s, (3 + i,)), (q_r, (3 + i,)), t)
            send((th, (2, r)), (th, (2, r)), (q_s, (5 + i,)), (q_r, (5 + i,)), sb)

    def q_rest():
        for i in range(2):
            got(th.at[2, r2, pl.ds(i * H, H)], q_r.at[3 + i])
        send((th, (2, r2)), (th, (2, r2)), (q_s, (7,)), (q_r, (7,)), sb)
        got(th.at[2, srow], q_r.at[2])
        got(th.at[2, sm], q_r.at[5])
        got(th.at[2, sp], q_r.at[6])
        got(th.at[2, s2], q_r.at[7])

    row_ids = lax.broadcasted_iota(jnp.int32, (MB, MB), 0)
    col_ids = lax.broadcasted_iota(jnp.int32, (MB, MB), 1)
    rlim = (MB // 4) * rt[blk]

    def own_r():
        pltpu.make_async_copy(r_in.at[:, 0], rin, loc.at[0]).wait()
        for b in range(2):
            v = jnp.where((row_ids < rlim) & (col_ids < rlim), rin[b], 0.0)
            rbuf[0, b] = v.T
            z_send(0, b, True)
            z_send(0, b, False)
        for i in range(8):
            own_theta(i).start()

    bond = lax.broadcasted_iota(jnp.int32, (16, MB), 0)

    def couple(k, acc):
        here = bond == pairs[k, 0]
        return [
            acc[b] + jnp.where(here & (pairs[k, 1] == 2 * row + b), coefs[k], 0.0) for b in range(2)
        ]

    llim = (MB // 4) * lt[blk]
    strip = 32

    def dress(h):
        @pl.loop(0, PIECE // strip)
        def _(s):
            first = pl.multiple_of(s * strip, strip)
            rows = lax.broadcasted_iota(jnp.int32, (strip, MB), 0) + first + h * PIECE
            cols = lax.broadcasted_iota(jnp.int32, (strip, MB), 1)
            keep = (rows < llim) & (cols < llim)
            acc = [jnp.zeros((strip, MB), F32) for _ in range(2)]
            for a in range(16):
                v = lall[h, a // 2, a % 2, pl.ds(first, strip), :]
                for b in range(2):
                    acc[b] = acc[b] + coup[b][a : a + 1] * v
            for b in range(2):
                v = jnp.where(keep, acc[b], 0.0)
                xbuf[0, h, b, pl.ds(first, strip), :] = v
                store_x(0, b, first + h * PIECE, strip, v)

    def dress_send(h):
        l_rest(h)
        dress(h)
        x_send(h)

    l_own(0)
    l_own(1)
    q_first()
    send_theta(0)
    own_r()
    coup = lax.fori_loop(0, pairs.shape[0], couple, [jnp.zeros((16, MB), F32)] * 2)
    split_r(0)
    l_forward(0)
    l_own(2)
    l_forward(1)
    l_own(3)
    send_theta(1)
    l_forward(2)
    zf(1,0)
    dress_send(0)
    zf(1,1)
    dress_send(1)
    l_forward(3)
    dress_send(2)
    sib_theta(0)
    q_own()
    x_forward(0)
    dress_send(3)
    x_forward(1)
    split_r(1)
    for i in range(8):
        own_theta(i).wait()

    def event1():
        split_r(2)
        x_forward(2)
        zf(2,0)
        zf(2,1)
        split_r(3)

    def event2():
        x_forward(3)
        send_theta(2)
        split_x(1)
        sib_theta_got(0)

    def event3():
        split_x(3)
        q_forward()
        sib_theta(1)
        send_theta(3)

    def event4():
        sib_theta_got(1)

    def event5():
        zf(3,0)
        zf(3,1)

    def event6():
        for h in range(PARTS):
            x_rest(h)
        split_x(2)
        q_rest()

    def event7():
        sib_theta(2)

    def event8():
        split_r(4)
        split_r(5)

    def event9():
        sib_theta_got(2)

    def event10():
        sib_theta(3)

    def event11():
        z_got(4,0,True)
        z_got(4,1,False)
        split_r(6)
        split_r(7)

    def event12():
        sib_theta_got(3)

    events = {1: event1, 2: event2, 3: event3, 4: event4, 5: event5, 6: event6, 7: event7, 8: event8, 9: event9, 10: event10, 11: event11, 12: event12}

    def out_copy(g, j):
        dx, pair = pick([a for a, _ in GROUPS], g), pick([h for _, h in GROUPS], g)
        d = pick(DIST, pair * TASKS + j)
        q = x * NZ + (z + d) % NZ
        return dx, q

    yn, yd, yf = (y + 1) % NY, (y + 3) % NY, (y + 2) % NY

    def stage3(g):
        got(f2.at[g, 0], f2_r.at[g, 0])
        got(f2.at[g, 1], f2_r.at[g, 1])
        fin[g] = part[g, c, y] + f2[g, 0] + f2[g, 1]
        for j in range(TASKS):
            dx, q = out_copy(g, j)

            @pl.when(dx == 0)
            def _():
                pltpu.make_async_copy(fin.at[g, j], o_ref.at[0, q], o_l.at[g, j]).start()

            @pl.when(dx != 0)
            def _():
                to = (row, ((x + dx) % NX) * NZ + z)
                rc(fin.at[g, j], o_ref.at[0, q], o_s.at[g, j], o_r.at[g, j], to).start()

    def stage2(g):
        got(f1.at[g, 0], f1_r.at[g, 0])
        part[g, c, yn, 0] = part[g, c, yn, 0] + f1[g, 0]
        rc(part.at[g, c, yn], f2.at[g, 0], f2_s.at[g, 0], f2_r.at[g, 0], yp).start()
        got(f1.at[g, 1], f1_r.at[g, 1])
        part[g, c, yd, 1] = part[g, c, yd, 1] + f1[g, 1]
        rc(part.at[g, c, yd], f2.at[g, 1], f2_s.at[g, 1], f2_r.at[g, 1], ym).start()

    def stage1(g):
        got(sib.at[g], p_r.at[g])
        part[g, c, yf] = part[g, c, yf] + sib[g, yf]
        rc(part.at[g, c, yf, 0], f1.at[g, 0], f1_s.at[g, 0], f1_r.at[g, 0], yp).start()
        rc(part.at[g, c, yf, 1], f1.at[g, 1], f1_s.at[g, 1], f1_r.at[g, 1], ym).start()
        for yy in (yn, yd, y):
            part[g, c, yy] = part[g, c, yy] + sib[g, yy]

    def compute(g):
        dx, pair = pick([a for a, _ in GROUPS], g), pick([h for _, h in GROUPS], g)

        wides = []
        for j in range(TASKS):
            thi, tlo = split(th[dx, pair * TASKS + j])
            p = dot(x3[dx], jnp.concatenate([thi, tlo, thi], axis=0))
            phi, plo = split(jnp.concatenate([p[:MB], p[MB:]], axis=1))
            wides.append(jnp.concatenate([phi, phi, plo], axis=1))
        for j in range(TASKS):
            o = dot(wides[j], r3[pair * TASKS + j])
            for s in range(8):
                part[g, s % 2, s // 2, j] = o[s * SLAB : (s + 1) * SLAB, :]

        rc(part.at[g, other], sib.at[g], p_s.at[g], p_r.at[g], sb).start()

    @pl.loop(0, NG + 7)
    def _(g):
        @pl.when(g >= 7)
        def _():
            stage3(g - 7)

        @pl.when((g >= 4) & (g < NG + 4))
        def _():
            stage2(g - 4)

        @pl.when((g >= 2) & (g < NG + 2))
        def _():
            stage1(g - 2)

        for i, event in events.items():
            pl.when(g == i)(event)

        @pl.when(g < NG)
        def _():
            compute(g)

    @pl.loop(0, NG)
    def _(g):
        sent(part.at[g, other], p_s.at[g])
        sent(part.at[g, c, yf, 0], f1_s.at[g, 0])
        sent(part.at[g, c, yf, 1], f1_s.at[g, 1])
        sent(part.at[g, c, yn], f2_s.at[g, 0])
        sent(part.at[g, c, yd], f2_s.at[g, 1])
        for j in range(TASKS):
            dx, q = out_copy(g, j)
            back = ((x + NX - dx) % NX) * NZ + q % NZ

            @pl.when(dx == 0)
            def _():
                pltpu.make_async_copy(fin.at[g, j], o_ref.at[0, q], o_l.at[g, j]).wait()

            @pl.when(dx != 0)
            def _():
                sent(fin.at[g, j], o_s.at[g, j])
                got(o_ref.at[0, back], o_r.at[g, j])

    for like, ss in sends:
        sent(view(like), view(ss))


def apply(pairs, coefs, lt, rt, theta, left_env, right_env):
    dma = pltpu.SemaphoreType.DMA
    return pl.pallas_call(
        kernel,
        out_shape=jax.ShapeDtypeStruct((1, NX * NZ, SLAB, MB), F32),
        in_specs=[pl.BlockSpec(memory_space=pltpu.SMEM)] * 4 + [pl.BlockSpec(memory_space=pl.ANY)] * 3,
        out_specs=pl.BlockSpec(memory_space=pl.ANY),
        scratch_shapes=[
            pltpu.VMEM((4, 8, MB, MB), F32),
            pltpu.VMEM((2, MB, MB), F32),
            pltpu.VMEM((8, 2, MB, MB), F32),
            pltpu.VMEM((8, 6 * MB, MB), BF16),
            pltpu.VMEM((PARTS, 8, 2, PIECE, MB), F32),
            pltpu.VMEM((4, PARTS, 2, PIECE, MB), F32),
            pltpu.VMEM((4, 2 * MB, 3 * MB), BF16),
            pltpu.VMEM((NG, 2, 4, TASKS, SLAB, MB), F32),
            pltpu.VMEM((NG, 4, TASKS, SLAB, MB), F32),
            pltpu.VMEM((NG, 2, SLAB, MB), F32),
            pltpu.VMEM((NG, 2, TASKS, SLAB, MB), F32),
            pltpu.VMEM((NG, TASKS, SLAB, MB), F32),
            dma((1 + PARTS,)), dma((8,)),
            dma((PARTS, 8)), dma((PARTS, 8)),
            dma((2, 4, 2)), dma((2, 4, 2)),
            dma((2, 4)), dma((2, 4)),
            dma((2, 4)), dma((2, 4)),
            dma((9,)), dma((9,)),
            dma((4, PARTS)), dma((4, PARTS)),
            dma((NG,)), dma((NG,)),
            dma((NG, 2)), dma((NG, 2)),
            dma((NG, 2)), dma((NG, 2)),
            dma((NG, TASKS)), dma((NG, TASKS)), dma((NG, TASKS)),
        ],
        compiler_params=pltpu.CompilerParams(
            collective_id=0, has_side_effects=True, vmem_limit_bytes=56 * 2**20
        ),
        name="hpsi",
    )(pairs, coefs, lt, rt, theta, left_env, right_env)


def per_device(theta, left_env, right_env, left_tiles, right_tiles, pairs, coefs):
    return apply(pairs, coefs, left_tiles, right_tiles, theta, left_env, right_env)


def solution(mesh):
    return jax.shard_map(
        per_device,
        mesh=mesh,
        in_specs=(
            P("blk", None, None, None),
            P("row", "blk", None, None),
            P("row", "blk", None, None),
            P(),
            P(),
            P(),
            P(),
        ),
        out_specs=P("blk", None, "row", None),
        check_vma=False,
    )
```
